128 devices in a mesh: col: 16 (over x, z_hi, core), row: 8 (over y, z_lo).
Axes of the slice: x: 4, y: 4, z: 4 (z_hi: 2, z_lo: 2; z = z_hi * 2 + z_lo), core: 2. Of those that a mesh axis runs over, the one named last changes fastest.
Arguments:
- act_values: bfloat16 [3072, 8192], P('col', 'row'), may hold values from -0.109375 to 0.109375
- act_exps: int32 [3072, 256], P('col', 'row'), may hold values from -2 to 0
- grad_values: bfloat16 [3072, 34816], P('row', 'col'), may hold values from -6 to 6
- grad_exps: int32 [3072, 1088], P('row', 'col'), may hold values from -2 to 0
- weight_values: bfloat16 [8192, 34816], P('row', 'col'), may hold values from -0.03125 to 0.03125
- weight_exps: int32 [8192, 1088], P('row', 'col'), may hold values from -2 to 0
Outputs:
- input_grad: bfloat16 [3072, 8192], P('col', 'row')
- weight_grad: bfloat16 [8192, 34816], P('row', 'col')
The draws below stay inside these ranges and needn't reach their ends.
All inputs are finite; a program needn't handle non-finite values.
Results may differ from the reference program's by a relative error of at most 0.0034.
Values may be sent and summed in bfloat16 or wider, within the bound.
A program may use at most 128 MiB of HBM per device.

```python
import jax
import jax.numpy as jnp

D = 8192
F = 34816
BLOCK = 32
TOKENS = 3072


def set_ends(array, key, smallest, top_value):
    place = [jax.random.randint(jax.random.fold_in(key, axis), (), 0, length) for axis, length in enumerate(array.shape)]
    widest = array.shape.index(max(array.shape))
    beside = place[:widest] + [(place[widest] + 1) % array.shape[widest]] + place[widest + 1:]
    return array.at[tuple(place)].set(smallest).at[tuple(beside)].set(top_value)


def level_of(stream_key, extent, split, low, top_value):
    level, own = 1.0, jax.random.fold_in(stream_key, 6)
    for axis_at, shards_of in split:
        heights = jnp.exp(jax.random.uniform(jax.random.fold_in(own, axis_at), (shards_of,), jnp.float32, low / len(split), top_value / len(split)))
        level = level * jnp.repeat(heights, extent[axis_at] // shards_of).reshape([-1 if axis == axis_at else 1 for axis in range(len(extent))])
    return level


def gaussian(rng, dims, spread, limit, shards=(), kind=jnp.bfloat16):
    level = level_of(rng, dims, shards, -0.22, 0.18) if shards else 1.0
    array = jax.random.normal(rng, dims, jnp.float32) * spread * level
    return jnp.minimum(jnp.maximum(array, -limit), limit).astype(kind)


def setup_inputs(seed: int = 0) -> dict:
    streams_of = jax.random.split(jax.random.key(seed), 7)
    act_values = gaussian(streams_of[0], (TOKENS, D), TOKENS ** -0.5, 0.109375, ((0, 16), (1, 8)))
    act_exps = set_ends(jax.random.randint(streams_of[1], (TOKENS, D // BLOCK), -2, 1), jax.random.fold_in(streams_of[1], 1), -2, 0).astype(jnp.int32)
    grad_values = gaussian(streams_of[2], (TOKENS, F), 1.0, 6.0, ((0, 8), (1, 16)))
    grad_exps = set_ends(jax.random.randint(streams_of[3], (TOKENS, F // BLOCK), -2, 1), jax.random.fold_in(streams_of[3], 1), -2, 0).astype(jnp.int32)
    weight_values = gaussian(streams_of[4], (D, F), F ** -0.5, 0.03125, ((0, 8), (1, 16)))
    weight_exps = set_ends(jax.random.randint(streams_of[5], (D, F // BLOCK), -2, 1), jax.random.fold_in(streams_of[5], 1), -2, 0).astype(jnp.int32)
    return {"act_values": act_values, "act_exps": act_exps, "grad_values": grad_values, "grad_exps": grad_exps, "weight_values": weight_values, "weight_exps": weight_exps}


def scale_blocks(values, exponents):
    height, breadth = values.shape
    factor = jnp.exp2(exponents.astype(jnp.float32)).astype(values.dtype)
    return (values.reshape(height, breadth // BLOCK, BLOCK) * factor[:, :, None]).reshape(height, breadth)


def reference(act_values, act_exps, grad_values, grad_exps, weight_values, weight_exps):
    activ = scale_blocks(act_values, act_exps)
    gradient = scale_blocks(grad_values, grad_exps)
    weights = scale_blocks(weight_values, weight_exps)
    input_grad = jnp.dot(gradient, weights.T, preferred_element_type=jnp.float32).astype(jnp.bfloat16)
    weight_grad = jnp.dot(activ.T, gradient, preferred_element_type=jnp.float32).astype(jnp.bfloat16)
    return input_grad, weight_grad
```

```python
import functools

import jax
import jax.numpy as jnp
from jax import lax
from jax.experimental import pallas as pl
from jax.experimental.pallas import tpu as pltpu
from jax.sharding import PartitionSpec as P

MESH = pl.DeviceIdType.MESH
BF16, F32 = jnp.bfloat16, jnp.float32
BLOCK = 32

OWN = [(0, 0, q) for q in range(4)]
UP = OWN + [(0, 1, 0), (0, 1, 2), (-1, 0, 0), (-1, 0, 2), (-1, 1, 0), (-1, 1, 2)]
DOWN = OWN + [(0, 1, 1), (0, 1, 3), (1, 0, 1), (1, 0, 3), (1, 1, 1), (1, 1, 3)]
ACROSS = OWN + [(-1, 0, 1), (-1, 0, 3), (1, 0, 0), (1, 0, 2)]
HALVES = [
    (0, 0, 0), (0, 0, 1),
    (-1, 0, 0), (1, 0, 0), (0, 1, 0),
    (-1, 0, 1), (1, 0, 1), (0, 1, 1),
    (-1, 1, 0), (-1, 1, 1),
    (2, 0, 0), (1, 1, 0),
    (2, 0, 1), (1, 1, 1),
    (2, 1, 0), (2, 1, 1),
]


def factors(exps, spread):
    scale = jnp.exp2(exps.astype(F32)).astype(BF16)
    return jnp.dot(scale, spread, preferred_element_type=F32).astype(BF16)


def spreader(groups):
    shape = (groups, groups * BLOCK)
    hit = lax.broadcasted_iota(jnp.int32, shape, 1) // BLOCK == lax.broadcasted_iota(jnp.int32, shape, 0)
    return jnp.where(hit, 1.0, 0.0).astype(BF16)


def kernel(
    av_hbm, ae_hbm, gv_hbm, ge_hbm, wv_hbm, we_hbm,
    ig_hbm, wg_hbm,
    g, at, w, acc, wout, ps, pr, xs, xr, cs, zs, zr, out, ge, we, ae, a_own, a_pair, spread,
    in_sem, g_send, g_recv, pair_send, pair_recv, at_send, at_recv, mix_send, mix_recv,
    ps_send, ps_recv, xs_send, xr_recv, z_send, z_recv, out_sem, wout_sem,
):
    col, row = lax.axis_index("col"), lax.axis_index("row")
    x, zh, core = col // 4, (col // 2) % 2, col % 2
    y, zl = row // 2, row % 2

    def at_xz(dx, dz):
        return (((x + dx + 4) % 4) * 4 + ((zh + dz) % 2) * 2 + core, row)

    def at_yz(dy, dz):
        return (col, ((y + dy + 4) % 4) * 2 + (zl + dz) % 2)

    mate = (col + 1 - 2 * core, row)
    up, down, across = at_yz(1, 0), at_yz(-1, 0), at_yz(0, 1)
    right, left, far, over = at_xz(1, 0), at_xz(3, 0), at_xz(2, 0), at_xz(0, 1)

    own = 2 * y + zl
    loads = [
        pltpu.make_async_copy(gv_hbm, g.at[own], in_sem.at[0]),
        pltpu.make_async_copy(ge_hbm, ge, in_sem.at[1]),
        pltpu.make_async_copy(av_hbm, a_own, in_sem.at[2]),
        pltpu.make_async_copy(ae_hbm, ae, in_sem.at[3]),
        pltpu.make_async_copy(wv_hbm, w, in_sem.at[4]),
        pltpu.make_async_copy(we_hbm, we, in_sem.at[5]),
    ]
    for load in loads:
        load.start()

    barrier = pltpu.get_barrier_semaphore()
    peers = (up, down, across, right, left, far, over, mate)
    for peer in peers:
        pl.semaphore_signal(barrier, inc=1, device_id=peer, device_id_type=MESH)

    spread[...] = spreader(spread.shape[0])

    def block(dy, dz):
        return 2 * ((y + dy + 4) % 4) + (zl + dz) % 2

    def g_copy(link, unit):
        dy, dz, q = (UP, DOWN, ACROSS)[link][unit]
        piece = g.at[block(dy, dz), :, pl.ds(48 * q, 48)]
        return pltpu.make_async_remote_copy(
            src_ref=piece, dst_ref=piece, send_sem=g_send.at[link, unit], recv_sem=g_recv.at[link, unit],
            device_id=(up, down, across)[link], device_id_type=MESH,
        )

    def links(unit):
        return [k for k in range(3) if unit < len((UP, DOWN, ACROSS)[k])]

    def g_issue(unit):
        for k in links(unit):
            g_copy(k, unit).start()

    def g_arrived(unit):
        for k in links(unit):
            dy, dz, q = (UP, DOWN, ACROSS)[k][unit]
            piece = g.at[block(dy + (-1, 1, 0)[k], dz + (0, 0, 1)[k]), :, pl.ds(48 * q, 48)]
            pltpu.make_async_remote_copy(
                src_ref=piece, dst_ref=piece, send_sem=g_send.at[k, unit], recv_sem=g_recv.at[k, unit],
                device_id=(up, down, across)[k], device_id_type=MESH,
            ).wait_recv()

    loads[0].wait()
    loads[1].wait()
    for q in range(4):
        rows = pl.ds(48 * q, 48)
        scale = factors(ge[:, rows].reshape(96, ge.shape[2]), spread[...])
        g[own, :, rows] = (g[own, :, rows].reshape(scale.shape) * scale).reshape(2, 48, scale.shape[1])
        if q == 0:
            pl.semaphore_wait(barrier, len(peers))
        if q < 2:
            g_issue(q)

    loads[2].wait()
    loads[3].wait()
    groups = ae.shape[1]
    a_own[...] = a_own[...] * factors(ae[...], spread[:groups, : groups * BLOCK])
    half = a_own.shape[1] // 2
    mine = pl.ds(pl.multiple_of(core * half, half), half)
    theirs = pl.ds(pl.multiple_of((1 - core) * half, half), half)
    pair = pltpu.make_async_remote_copy(
        src_ref=a_own.at[:, theirs], dst_ref=a_pair.at[core], send_sem=pair_send, recv_sem=pair_recv,
        device_id=mate, device_id_type=MESH,
    )
    pair.start()
    a_pair[core] = a_own[:, mine]

    loads[4].wait()
    loads[5].wait()

    def scale_weight(i, carry):
        rows = pl.ds(pl.multiple_of(i * 128, 128), 128)
        w[rows] = w[rows] * factors(we[rows], spread[...])
        return carry

    lax.fori_loop(0, w.shape[0] // 128, scale_weight, 0)

    pair.wait()
    at[2 * x + zh, mine] = a_pair[...].reshape(2 * a_pair.shape[1], half).T

    def at_copy(dx, dz, k, device):
        piece = at.at[2 * ((x + dx) % 4) + (zh + dz) % 2, mine]
        return pltpu.make_async_remote_copy(
            src_ref=piece, dst_ref=piece, send_sem=at_send.at[k], recv_sem=at_recv.at[k],
            device_id=device, device_id_type=MESH,
        )

    def mix_copy(dx, dz, to_me=False):
        k = 2 * dx + dz
        piece = at.at[2 * ((x + dx) % 4) + (zh + dz) % 2, theirs if to_me else mine]
        return pltpu.make_async_remote_copy(
            src_ref=piece, dst_ref=piece, send_sem=mix_send.at[k], recv_sem=mix_recv.at[k],
            device_id=mate, device_id_type=MESH,
        )

    at_sent = [at_copy(0, 0, 0, over)] + [at_copy(0, 0, d, at_xz(d, 0)) for d in (1, 3, 2)]
    for copy in at_sent:
        copy.start()
    mixed = [mix_copy(0, 0)]
    mixed[0].start()

    def at_over():
        at_copy(0, 1, 0, over).wait_recv()
        for d in (1, 3, 2):
            at_sent.append(at_copy(0, 1, 3 + d, at_xz(d, 0)))
            at_sent[-1].start()
        mixed.append(mix_copy(0, 1))
        mixed[-1].start()

    def at_line(dz):
        for d in (1, 3, 2):
            at_copy(4 - d, dz, 3 * dz + d, right).wait_recv()
            mixed.append(mix_copy(4 - d, dz))
            mixed[-1].start()

    def at_whole():
        for dx in range(4):
            for dz in range(2):
                mix_copy(dx, dz, True).wait_recv()

    def target(k):
        dy, dz, _ = HALVES[k]
        return (y + dy + 4) % 4, (zl + dz) % 2

    def ps_copy(k):
        slot = k % 4
        return pltpu.make_async_remote_copy(
            src_ref=ps.at[slot, 1 - core], dst_ref=pr.at[slot], send_sem=ps_send.at[slot], recv_sem=ps_recv.at[slot],
            device_id=mate, device_id_type=MESH,
        )

    def xs_copy(k):
        xt, zt = target(k)
        h = HALVES[k][2]
        apart = (x - xt + 4) % 4
        return pltpu.make_async_remote_copy(
            src_ref=xs.at[k % 4], dst_ref=xr.at[zt, (apart + 3) % 4, h], send_sem=xs_send.at[k % 4],
            recv_sem=xr_recv.at[zt, (apart + 3) % 4, h],
            device_id=(xt * 4 + zh * 2 + core, row), device_id_type=MESH,
        )

    def z_copy(h):
        return pltpu.make_async_remote_copy(
            src_ref=zs.at[h], dst_ref=zr.at[h], send_sem=z_send.at[h], recv_sem=z_recv.at[h],
            device_id=over, device_id_type=MESH,
        )

    def compute(k):
        dy, dz, h = HALVES[k]
        if k >= 4:
            ps_copy(k - 4).wait_send()
        b = block(dy, dz)

        def tile(n, carry):
            rows = pl.ds(pl.multiple_of(n * 256, 256), 256)
            part = lax.dot_general(
                g[b, :, pl.ds(96 * h, 96)].reshape(192, g.shape[3]), w[rows], (((1,), (1,)), ((), ())),
                preferred_element_type=F32,
            )
            ps[k % 4, :, :, rows] = part.reshape(2, 96, 256)
            return carry

        lax.fori_loop(0, w.shape[0] // 256, tile, 0)
        ps_copy(k).start()

    def consume(k):
        h = HALVES[k][2]
        xt, zt = target(k)
        ps_copy(k).wait_recv()

        @pl.when(xt == x)
        def _():
            cs[zt, h] = ps[k % 4, core] + pr[k % 4]

        if k >= 4:
            @pl.when(target(k - 4)[0] != x)
            def _():
                xs_copy(k - 4).wait_send()

        @pl.when(xt != x)
        def _():
            xs[k % 4] = (ps[k % 4, core] + pr[k % 4]).astype(BF16)
            xs_copy(k).start()

    def collect(k):
        h = HALVES[k][2]
        xt, zt = target(k)

        @pl.when(xt == x)
        def _():
            for j in range(3):
                pltpu.make_async_remote_copy(
                    src_ref=xs.at[0], dst_ref=xr.at[zt, j, h], send_sem=xs_send.at[0], recv_sem=xr_recv.at[zt, j, h],
                    device_id=right, device_id_type=MESH,
                ).wait_recv()
            total = (cs[zt, h] + xr[zt, 0, h].astype(F32)) + (xr[zt, 1, h].astype(F32) + xr[zt, 2, h].astype(F32))

            @pl.when(zt == zh)
            def _():
                cs[zt, h] = total

            @pl.when(zt != zh)
            def _():
                zs[h] = total.astype(BF16)
                z_copy(h).start()

    def tiles(dy, dz, count, first, last, low, high):
        b = block(dy, dz) if count == 1 else 2 * ((y + dy + 4) % 4)

        def part(cols, size):
            if count == 1:
                lhs = at[b]
            else:
                lhs = jnp.concatenate([at[b], at[b + 1]], axis=1)
            rhs = g[pl.ds(b, count), :, :, cols].reshape(count * 384, size)
            value = jnp.dot(lhs, rhs, preferred_element_type=F32)
            if not first:
                value = acc[:, cols] + value
            if last:
                wout[:, cols] = value.astype(BF16)
            else:
                acc[:, cols] = value

        def tile(n, carry):
            part(pl.ds(pl.multiple_of(n * 256, 256), 256), 256)
            return carry

        full = g.shape[3] // 256
        lax.fori_loop(low, min(high, full), tile, 0)
        if high > full:
            part(pl.ds(full * 256, g.shape[3] - full * 256), g.shape[3] - full * 256)

    def wout_copy(i):
        cols = (pl.ds(0, 1024), pl.ds(1024, 1152))[i]
        return pltpu.make_async_copy(wout.at[:, cols], wg_hbm.at[:, cols], wout_sem.at[i])

    compute(0)
    compute(1)
    consume(0)
    consume(1)
    g_arrived(0)
    g_issue(2)
    at_over()
    g_arrived(1)
    g_issue(3)
    compute(2)
    compute(3)
    consume(2)
    compute(4)
    consume(3)
    at_line(0)
    collect(0)
    collect(1)
    consume(4)
    g_arrived(2)
    g_issue(4)
    g_arrived(3)
    g_issue(5)
    compute(5)
    compute(6)
    consume(5)
    compute(7)
    consume(6)
    collect(2)
    collect(3)
    collect(4)
    consume(7)
    g_arrived(4)
    g_issue(6)
    compute(8)
    at_line(1)
    consume(8)
    g_arrived(5)
    g_issue(7)
    compute(9)
    at_whole()
    consume(9)
    collect(5)
    collect(6)
    collect(7)
    tiles(0, 0, 2, True, False, 0, 9)
    g_arrived(6)
    g_issue(8)
    compute(10)
    compute(11)
    consume(10)
    tiles(-1, 0, 2, False, False, 0, 4)
    consume(11)
    collect(8)
    collect(9)
    tiles(-1, 0, 2, False, False, 4, 9)
    g_arrived(7)
    g_issue(9)
    compute(12)
    compute(13)
    consume(12)
    tiles(1, 0, 2, False, False, 0, 4)
    consume(13)
    collect(10)
    collect(11)
    tiles(1, 0, 2, False, False, 4, 9)
    g_arrived(8)
    compute(14)
    tiles(2, 0, 1, False, False, 0, 4)
    consume(14)
    collect(12)
    collect(13)
    tiles(2, 0, 1, False, False, 4, 9)
    g_arrived(9)
    compute(15)
    tiles(2, 1, 1, False, True, 0, 4)
    consume(15)
    wout_copy(0).start()
    collect(14)
    tiles(2, 1, 1, False, True, 4, 9)
    wout_copy(1).start()
    collect(15)
    for h in range(2):
        z_copy(h).wait_recv()
        out[:, pl.ds(96 * h, 96)] = (cs[zh, h] + zr[h].astype(F32)).astype(BF16).reshape(1, 96, out.shape[2])
    final = pltpu.make_async_copy(out, ig_hbm, out_sem)
    final.start()

    for unit in range(10):
        for k in links(unit):
            g_copy(k, unit).wait_send()
    for copy in at_sent + mixed:
        copy.wait_send()
    for k in range(12, 16):
        ps_copy(k).wait_send()

        @pl.when(target(k)[0] != x)
        def _():
            xs_copy(k).wait_send()

    for h in range(2):
        z_copy(h).wait_send()
    for i in range(2):
        wout_copy(i).wait()
    final.wait()


def shards(act_values, act_exps, grad_values, grad_exps, weight_values, weight_exps):
    tokens, model = act_values.shape
    rows, width = grad_values.shape
    groups = width // BLOCK
    dma = pltpu.SemaphoreType.DMA
    scratch = [
        pltpu.VMEM((8, 2, rows // 2, width), BF16),
        pltpu.VMEM((8, model, rows), BF16),
        pltpu.VMEM((model, width), BF16),
        pltpu.VMEM((model, width), F32),
        pltpu.VMEM((model, width), BF16),
        pltpu.VMEM((4, 2, rows // 4, model), F32),
        pltpu.VMEM((4, rows // 4, model), F32),
        pltpu.VMEM((4, rows // 4, model), BF16),
        pltpu.VMEM((2, 3, 2, rows // 4, model), BF16),
        pltpu.VMEM((2, 2, rows // 4, model), F32),
        pltpu.VMEM((2, rows // 4, model), BF16),
        pltpu.VMEM((2, rows // 4, model), BF16),
        pltpu.VMEM((1, tokens, model), BF16),
        pltpu.VMEM((2, rows // 2, groups), jnp.int32),
        pltpu.VMEM((model, groups), jnp.int32),
        pltpu.VMEM((tokens, model // BLOCK), jnp.int32),
        pltpu.VMEM((tokens, model), BF16),
        pltpu.VMEM((2, tokens, model // 2), BF16),
        pltpu.VMEM((groups, width), BF16),
        dma((6,)),
        dma((3, 10)), dma((3, 10)),
        dma, dma,
        dma((7,)), dma((7,)),
        dma((8,)), dma((8,)),
        dma((4,)), dma((4,)),
        dma((4,)), dma((2, 3, 2)),
        dma((2,)), dma((2,)),
        dma, dma((2,)),
    ]
    anywhere = pl.BlockSpec(memory_space=pl.ANY)
    input_grad, weight_grad = pl.pallas_call(
        kernel,
        out_shape=(
            jax.ShapeDtypeStruct((1, tokens, model), BF16),
            jax.ShapeDtypeStruct((model, width), BF16),
        ),
        in_specs=[anywhere] * 6,
        out_specs=(anywhere, anywhere),
        scratch_shapes=scratch,
        compiler_params=pltpu.CompilerParams(
            collective_id=0, has_side_effects=True, vmem_limit_bytes=60 * 2**20
        ),
        cost_estimate=pl.CostEstimate(
            flops=4 * 8 * rows * model * width, bytes_accessed=16 * 2**20, transcendentals=0
        ),
        name="fused",
    )(
        act_values, act_exps,
        grad_values.reshape(2, rows // 2, width), grad_exps.reshape(2, rows // 2, groups),
        weight_values, weight_exps,
    )
    return input_grad.reshape(tokens, model), weight_grad


def solution(mesh):
    in_specs = (P("col", "row"),) * 2 + (P("row", "col"),) * 4
    out_specs = (P("col", "row"), P("row", "col"))
    return jax.shard_map(shards, mesh=mesh, in_specs=in_specs, out_specs=out_specs, check_vma=False)
```

```python
import functools

import jax
import jax.numpy as jnp
from jax import lax
from jax.experimental import pallas as pl
from jax.experimental.pallas import tpu as pltpu
from jax.sharding import PartitionSpec as P

MESH = pl.DeviceIdType.MESH
BF16, F32 = jnp.bfloat16, jnp.float32
BLOCK = 32

SIZES = (64, 64, 32, 32)
OFFS = (0, 64, 128, 160)
OWN = [(0, 0, q) for q in range(4)]
UP = OWN + [(0, 1, 1), (-1, 0, 0), (0, 1, 3), (-1, 1, 1), (-1, 0, 2), (-1, 1, 3)]
DOWN = OWN + [(0, 1, 1), (1, 0, 1), (1, 0, 3), (1, 1, 0), (1, 1, 2), (0, 1, 3)]
ACROSS = OWN + [(1, 0, 0), (1, 0, 2), (-1, 0, 0), (-1, 0, 2)]
LINKS = (UP, DOWN, ACROSS)
JOBS = [
    [(0, 0, 0), (0, 0, 1)],
    [(0, 0, 2), (0, 0, 3)],
    [(-1, 0, 0), (-1, 0, 1)],
    [(1, 0, 0), (1, 0, 1)],
    [(-1, 0, 2), (-1, 0, 3), (1, 0, 2), (1, 0, 3)],
    [(0, 1, 0), (0, 1, 1)],
    [(0, 1, 2), (0, 1, 3), (-1, 1, 1)],
    [(2, 0, 0), (2, 0, 1)],
    [(1, 1, 1), (1, 1, 0)],
    [(-1, 1, 3), (2, 0, 3), (1, 1, 2)],
    [(2, 1, 1), (2, 1, 0)],
    [(2, 0, 2), (2, 1, 2), (-1, 1, 0)],
    [(2, 1, 3), (1, 1, 3), (-1, 1, 2)],
]


def factors(exps, spread):
    scale = jnp.exp2(exps.astype(F32)).astype(BF16)
    return lax.dot_general(scale, spread, (((0,), (0,)), ((), ())), preferred_element_type=F32).astype(BF16)


def spreader(groups):
    shape = (groups, groups * BLOCK)
    hit = lax.broadcasted_iota(jnp.int32, shape, 1) // BLOCK == lax.broadcasted_iota(jnp.int32, shape, 0)
    return jnp.where(hit, 1.0, 0.0).astype(BF16)


def kernel(
    av_hbm, ae_hbm, gv_hbm, ge_hbm, wv_hbm, we_hbm,
    out, wout,
    g, at, w, acc, ps, pr, xs, xr, cs, zs, zr, ge, we, ae, a_own, a_pair, spread,
    in_sem, g_send, g_recv, pair_send, pair_recv, at_send, at_recv, mix_send, mix_recv,
    ps_send, ps_recv, xs_send, xr_recv, z_send, z_recv,
):
    col, row = lax.axis_index("col"), lax.axis_index("row")
    x, zh, core = col // 4, (col // 2) % 2, col % 2
    y, zl = row // 2, row % 2

    def at_xz(dx, dz):
        return (((x + dx + 4) % 4) * 4 + ((zh + dz) % 2) * 2 + core, row)

    def at_yz(dy, dz):
        return (col, ((y + dy + 4) % 4) * 2 + (zl + dz) % 2)

    mate = (col + 1 - 2 * core, row)
    up, down, across = at_yz(1, 0), at_yz(-1, 0), at_yz(0, 1)
    right, left, far, over = at_xz(1, 0), at_xz(3, 0), at_xz(2, 0), at_xz(0, 1)

    own = 2 * y + zl
    loads = [
        pltpu.make_async_copy(gv_hbm, g.at[own], in_sem.at[0]),
        pltpu.make_async_copy(ge_hbm, ge, in_sem.at[1]),
        pltpu.make_async_copy(av_hbm, a_own, in_sem.at[2]),
        pltpu.make_async_copy(ae_hbm, ae, in_sem.at[3]),
        pltpu.make_async_copy(wv_hbm, w, in_sem.at[4]),
        pltpu.make_async_copy(we_hbm, we, in_sem.at[5]),
    ]
    for load in loads:
        load.start()

    barrier = pltpu.get_barrier_semaphore()
    peers = (up, down, across, right, left, far, over, mate)
    for peer in peers:
        pl.semaphore_signal(barrier, inc=1, device_id=peer, device_id_type=MESH)

    spread[...] = spreader(spread.shape[0])

    def block(dy, dz):
        return 2 * ((y + dy + 4) % 4) + (zl + dz) % 2

    def rows_of(q):
        return pl.ds(OFFS[q], SIZES[q])

    def g_copy(link, unit, arriving=False):
        dy, dz, q = LINKS[link][unit]
        if arriving:
            dy, dz = dy + (-1, 1, 0)[link], dz + (0, 0, 1)[link]
        piece = g.at[block(dy, dz), :, rows_of(q)]
        return pltpu.make_async_remote_copy(
            src_ref=piece, dst_ref=piece, send_sem=g_send.at[link, unit], recv_sem=g_recv.at[link, unit],
            device_id=(up, down, across)[link], device_id_type=MESH,
        )

    def g_issue(y_unit=None, z_unit=None):
        for link, unit in ((0, y_unit), (1, y_unit), (2, z_unit)):
            if unit is not None:
                g_copy(link, unit).start()

    def g_arrived(y_unit=None, z_unit=None):
        for link, unit in ((0, y_unit), (1, y_unit), (2, z_unit)):
            if unit is not None:
                g_copy(link, unit, True).wait_recv()

    loads[0].wait()
    loads[1].wait()
    scale = factors(ge[...], spread[...])
    g[own] = (g[own].reshape(scale.shape) * scale).reshape(g.shape[1:])
    pl.semaphore_wait(barrier, len(peers))
    g_issue(0, 0)
    g_issue(1, 1)

    loads[2].wait()
    loads[3].wait()
    groups = ae.shape[0]
    a_own[...] = a_own[...] * factors(ae[...], spread[:groups, : groups * BLOCK])
    half = a_own.shape[1] // 2
    mine = pl.ds(pl.multiple_of(core * half, half), half)
    theirs = pl.ds(pl.multiple_of((1 - core) * half, half), half)
    pair = pltpu.make_async_remote_copy(
        src_ref=a_own.at[:, theirs], dst_ref=a_pair.at[core], send_sem=pair_send, recv_sem=pair_recv,
        device_id=mate, device_id_type=MESH,
    )
    pair.start()
    a_pair[core] = a_own[:, mine]

    loads[4].wait()
    loads[5].wait()

    def scale_weight(i, carry):
        rows = pl.ds(pl.multiple_of(i * 128, 128), 128)
        w[rows] = w[rows] * factors(we[:, rows], spread[...])
        return carry

    lax.fori_loop(0, w.shape[0] // 128, scale_weight, 0)

    pair.wait()
    at[2 * x + zh, mine] = a_pair[...].reshape(2 * a_pair.shape[1], half).T

    def at_copy(dx, dz, k, device):
        piece = at.at[2 * ((x + dx) % 4) + (zh + dz) % 2, mine]
        return pltpu.make_async_remote_copy(
            src_ref=piece, dst_ref=piece, send_sem=at_send.at[k], recv_sem=at_recv.at[k],
            device_id=device, device_id_type=MESH,
        )

    def mix_copy(dx, dz, to_me=False):
        k = 2 * dx + dz
        piece = at.at[2 * ((x + dx) % 4) + (zh + dz) % 2, theirs if to_me else mine]
        return pltpu.make_async_remote_copy(
            src_ref=piece, dst_ref=piece, send_sem=mix_send.at[k], recv_sem=mix_recv.at[k],
            device_id=mate, device_id_type=MESH,
        )

    at_sent = [at_copy(0, 0, 0, over)] + [at_copy(0, 0, d, at_xz(d, 0)) for d in (1, 3, 2)]
    for copy in at_sent:
        copy.start()
    mixed = [mix_copy(0, 0)]
    mixed[0].start()

    def at_over():
        at_copy(0, 1, 0, over).wait_recv()
        for d in (1, 3, 2):
            at_sent.append(at_copy(0, 1, 3 + d, at_xz(d, 0)))
            at_sent[-1].start()
        mixed.append(mix_copy(0, 1))
        mixed[-1].start()

    def at_line(dz):
        for d in (1, 3, 2):
            at_copy(4 - d, dz, 3 * dz + d, right).wait_recv()
            mixed.append(mix_copy(4 - d, dz))
            mixed[-1].start()

    def at_whole():
        for dx in range(4):
            for dz in range(2):
                mix_copy(dx, dz, True).wait_recv()

    def target(piece):
        return (y + piece[0] + 4) % 4, (zl + piece[1]) % 2

    def size_of(k):
        return sum(SIZES[piece[2]] for piece in JOBS[k])

    def pieces_of(k):
        start = 0
        for i, piece in enumerate(JOBS[k]):
            yield i, piece, pl.ds(start, SIZES[piece[2]])
            start += SIZES[piece[2]]

    def ps_copy(k):
        slot, rows = k % 4, pl.ds(0, size_of(k))
        return pltpu.make_async_remote_copy(
            src_ref=ps.at[slot, 1 - core, rows], dst_ref=pr.at[slot, rows],
            send_sem=ps_send.at[slot], recv_sem=ps_recv.at[slot], device_id=mate, device_id_type=MESH,
        )

    def xs_copy(k, i, piece, rows):
        xt, zt = target(piece)
        seat, q = (x - xt + 3) % 4, piece[2]
        return pltpu.make_async_remote_copy(
            src_ref=xs.at[k % 4, rows], dst_ref=xr.at[zt, seat, rows_of(q)],
            send_sem=xs_send.at[k % 4, i], recv_sem=xr_recv.at[zt, seat, q],
            device_id=(xt * 4 + zh * 2 + core, row), device_id_type=MESH,
        )

    def z_copy(q):
        return pltpu.make_async_remote_copy(
            src_ref=zs.at[rows_of(q)], dst_ref=zr.at[rows_of(q)], send_sem=z_send.at[q], recv_sem=z_recv.at[q],
            device_id=over, device_id_type=MESH,
        )

    def compute(k):
        if k >= 4:
            ps_copy(k - 4).wait_send()
        total = size_of(k)

        def tile(n, carry):
            cols = pl.ds(pl.multiple_of(n * 256, 256), 256)
            parts = [g[block(dy, dz), :, rows_of(q)] for dy, dz, q in JOBS[k]]
            lhs = jnp.concatenate(parts, axis=1).reshape(2 * total, g.shape[3])
            part = lax.dot_general(lhs, w[cols], (((1,), (1,)), ((), ())), preferred_element_type=F32)
            ps[k % 4, :, pl.ds(0, total), cols] = part.reshape(2, total, 256)
            return carry

        lax.fori_loop(0, w.shape[0] // 256, tile, 0)
        ps_copy(k).start()

    def xs_sent(k):
        for i, piece, rows in pieces_of(k):
            @pl.when(target(piece)[0] != x)
            def _():
                xs_copy(k, i, piece, rows).wait_send()

    def consume(k):
        ps_copy(k).wait_recv()
        if k >= 4:
            xs_sent(k - 4)
        for i, piece, rows in pieces_of(k):
            xt, zt = target(piece)

            @pl.when(xt == x)
            def _():
                cs[zt, rows_of(piece[2])] = ps[k % 4, core, rows] + pr[k % 4, rows]

            @pl.when(xt != x)
            def _():
                xs[k % 4, rows] = (ps[k % 4, core, rows] + pr[k % 4, rows]).astype(BF16)
                xs_copy(k, i, piece, rows).start()

    def collect(k):
        for _, piece, _ in pieces_of(k):
            collect_piece(piece)

    def collect_piece(piece):
        q = piece[2]
        xt, zt = target(piece)
        rows = rows_of(q)

        @pl.when(xt == x)
        def _():
            for j in range(3):
                pltpu.make_async_remote_copy(
                    src_ref=xs.at[0, pl.ds(0, SIZES[q])], dst_ref=xr.at[zt, j, rows], send_sem=xs_send.at[0, 0],
                    recv_sem=xr_recv.at[zt, j, q], device_id=right, device_id_type=MESH,
                ).wait_recv()
            total = (cs[zt, rows] + xr[zt, 0, rows].astype(F32)) + (
                xr[zt, 1, rows].astype(F32) + xr[zt, 2, rows].astype(F32)
            )

            @pl.when(zt == zh)
            def _():
                cs[zt, rows] = total

            @pl.when(zt != zh)
            def _():
                zs[rows] = total.astype(BF16)
                z_copy(q).start()

    def tiles(pairs, first, last, low, high):
        blocks = [block(dy, dz) for dy, dz in pairs]
        depth = len(blocks) * g.shape[1] * g.shape[2]

        def part(cols, size):
            lhs = jnp.concatenate([at[b] for b in blocks], axis=1)
            rhs = jnp.concatenate([g[b, :, :, cols] for b in blocks], axis=0).reshape(depth, size)
            value = jnp.dot(lhs, rhs, preferred_element_type=F32)
            if not first:
                value = acc[:, cols] + value
            if last:
                wout[:, cols] = value.astype(BF16)
            else:
                acc[:, cols] = value

        def tile(n, carry):
            part(pl.ds(pl.multiple_of(n * 256, 256), 256), 256)
            return carry

        full = g.shape[3] // 256
        lax.fori_loop(low, min(high, full), tile, 0)
        if high > full:
            part(pl.ds(full * 256, g.shape[3] - full * 256), g.shape[3] - full * 256)

    compute(0)
    compute(1)
    consume(0)
    consume(1)
    g_arrived(0)
    g_issue(2)
    g_arrived(1, 0)
    g_issue(3, 2)
    compute(2)
    compute(3)
    consume(2)
    consume(3)
    at_over()
    g_arrived(2, 1)
    g_issue(4, 3)
    g_arrived(3, 2)
    g_issue(5, 4)
    compute(4)
    compute(5)
    consume(4)
    at_line(0)
    consume(5)
    collect(0)
    collect(1)
    g_arrived(4, 3)
    g_issue(6, 5)
    compute(6)
    collect(2)
    collect(3)
    consume(6)
    g_arrived(5, 4)
    g_issue(7, 6)
    compute(7)
    compute(8)
    consume(7)
    at_line(1)
    consume(8)
    collect(4)
    collect(5)
    g_arrived(6, 5)
    g_issue(8, 7)
    compute(9)
    at_whole()
    consume(9)
    collect(6)
    tiles([(0, 0), (0, 1)], True, False, 0, 9)
    g_arrived(7)
    g_issue(9)
    compute(10)
    collect(7)
    consume(10)
    tiles([(-1, 0), (1, 0)], False, False, 0, 9)
    g_arrived(8, 6)
    compute(11)
    collect(8)
    collect(9)
    consume(11)
    g_arrived(9, 7)
    compute(12)
    collect(10)
    rest = [(1, 1), (2, 0), (-1, 1), (2, 1)]
    tiles(rest, False, True, 0, 2)
    consume(12)
    tiles(rest, False, True, 2, 5)
    collect(11)
    tiles(rest, False, True, 5, 8)
    collect(12)
    tiles(rest, False, True, 8, 9)
    for q in range(4):
        z_copy(q).wait_recv()
        out[0, rows_of(q)] = (cs[zh, rows_of(q)] + zr[rows_of(q)].astype(F32)).astype(BF16)

    for link, units in enumerate(LINKS):
        for unit in range(len(units)):
            g_copy(link, unit).wait_send()
    for copy in at_sent + mixed:
        copy.wait_send()
    for k in range(len(JOBS) - 4, len(JOBS)):
        ps_copy(k).wait_send()
        xs_sent(k)
    for q in range(4):
        z_copy(q).wait_send()


def shards(act_values, act_exps, grad_values, grad_exps, weight_values, weight_exps):
    tokens, model = act_values.shape
    rows, width = grad_values.shape
    groups = width // BLOCK
    dma = pltpu.SemaphoreType.DMA
    scratch = [
        pltpu.VMEM((8, 2, rows // 2, width), BF16),
        pltpu.VMEM((8, model, rows), BF16),
        pltpu.VMEM((model, width), BF16),
        pltpu.VMEM((model, width), F32),
        pltpu.VMEM((4, 2, 128, model), F32),
        pltpu.VMEM((4, 128, model), F32),
        pltpu.VMEM((4, 128, model), BF16),
        pltpu.VMEM((2, 3, rows // 2, model), BF16),
        pltpu.VMEM((2, rows // 2, model), F32),
        pltpu.VMEM((rows // 2, model), BF16),
        pltpu.VMEM((rows // 2, model), BF16),
        pltpu.VMEM((groups, rows), jnp.int32),
        pltpu.VMEM((groups, model), jnp.int32),
        pltpu.VMEM((model // BLOCK, tokens), jnp.int32),
        pltpu.VMEM((tokens, model), BF16),
        pltpu.VMEM((2, tokens, model // 2), BF16),
        pltpu.VMEM((groups, width), BF16),
        dma((6,)),
        dma((3, 10)), dma((3, 10)),
        dma, dma,
        dma((7,)), dma((7,)),
        dma((8,)), dma((8,)),
        dma((4,)), dma((4,)),
        dma((4, 4)), dma((2, 3, 4)),
        dma((4,)), dma((4,)),
    ]
    anywhere = pl.BlockSpec(memory_space=pl.ANY)
    input_grad, weight_grad = pl.pallas_call(
        kernel,
        out_shape=(pltpu.VMEM((1, tokens, model), BF16), pltpu.VMEM((model, width), BF16)),
        in_specs=[anywhere] * 6,
        out_specs=(pl.BlockSpec(memory_space=pltpu.VMEM),) * 2,
        scratch_shapes=scratch,
        compiler_params=pltpu.CompilerParams(
            collective_id=0, has_side_effects=True, vmem_limit_bytes=56 * 2**20
        ),
        cost_estimate=pl.CostEstimate(
            flops=4 * 8 * rows * model * width, bytes_accessed=16 * 2**20, transcendentals=0
        ),
        name="fused",
    )(
        act_values, act_exps.T,
        grad_values.reshape(2, rows // 2, width), grad_exps.T,
        weight_values, weight_exps.T,
    )
    return input_grad.reshape(tokens, model), weight_grad


def solution(mesh):
    in_specs = (P("col", "row"),) * 2 + (P("row", "col"),) * 4
    out_specs = (P("col", "row"), P("row", "col"))
    return jax.shard_map(shards, mesh=mesh, in_specs=in_specs, out_specs=out_specs, check_vma=False)
```

```python
import functools

import jax
import jax.numpy as jnp
from jax import lax
from jax.experimental import pallas as pl
from jax.experimental.pallas import tpu as pltpu
from jax.sharding import PartitionSpec as P

MESH = pl.DeviceIdType.MESH
BF16, F32 = jnp.bfloat16, jnp.float32
BLOCK = 32

SIZES = (64, 32, 64, 32, 16, 16, 16, 16, 48, 16, 48, 16)
OFFS = (0, 64, 96, 160, 160, 176, 64, 80, 96, 144, 0, 48)
UP = [
    (0, 0, 0), (0, 0, 1), (0, 0, 2), (0, 0, 3), (0, 1, 0), (-1, 0, 0), (-1, 1, 0), (-1, 1, 1), (-1, 0, 1),
    (0, 1, 4), (0, 1, 5),
]
DOWN = [
    (0, 0, 0), (0, 0, 2), (0, 0, 1), (0, 0, 3), (0, 1, 2), (1, 0, 2), (1, 1, 2), (1, 1, 3), (1, 0, 3),
    (0, 1, 6), (0, 1, 7),
]
ACROSS = [
    (0, 0, 0), (0, 0, 2), (0, 0, 1), (0, 0, 3), (-1, 0, 1), (1, 0, 3), (1, 0, 10), (-1, 0, 8), (1, 0, 11),
    (-1, 0, 9),
]
LINKS = (UP, DOWN, ACROSS)
JOBS = [
    [(0, 0, 0), (0, 0, 1), (0, 0, 3)],
    [(0, 0, 2), (-1, 0, 0)],
    [(1, 0, 0), (1, 0, 2)],
    [(-1, 0, 1), (-1, 0, 2), (1, 0, 1)],
    [(0, 1, 0), (0, 1, 2)],
    [(-1, 0, 3), (1, 0, 3), (0, 1, 1)],
    [(-1, 1, 0), (1, 1, 2)],
    [(2, 0, 0), (2, 0, 2)],
    [(0, 1, 3), (-1, 1, 1), (1, 1, 3)],
    [(2, 1, 0), (2, 1, 2)],
    [(2, 1, 1), (2, 1, 3), (1, 1, 10)],
    [(2, 0, 1), (2, 0, 3), (-1, 1, 8)],
    [(-1, 1, 4), (1, 1, 6), (1, 1, 11)],
    [(-1, 1, 5), (1, 1, 7), (-1, 1, 9)],
]


def factors(exps, spread):
    scale = jnp.exp2(exps.astype(F32)).astype(BF16)
    return lax.dot_general(scale, spread, (((0,), (0,)), ((), ())), preferred_element_type=F32).astype(BF16)


def spreader(groups):
    shape = (groups, groups * BLOCK)
    hit = lax.broadcasted_iota(jnp.int32, shape, 1) // BLOCK == lax.broadcasted_iota(jnp.int32, shape, 0)
    return jnp.where(hit, 1.0, 0.0).astype(BF16)


def kernel(
    av_hbm, ae_hbm, gv_hbm, ge_hbm, wv_hbm, we_hbm,
    out, wout,
    g, at, w, acc, ps, pr, xs, xr, rr, hs, cs, zs, zr, ge, we, ae, a_own, a_pair, spread,
    in_sem, g_send, g_recv, pair_send, pair_recv, at_send, at_recv, mix_send, mix_recv,
    ps_send, ps_recv, xs_send, xr_recv, rr_recv, rs_send, z_send, z_recv,
):
    col, row = lax.axis_index("col"), lax.axis_index("row")
    x, zh, core = col // 4, (col // 2) % 2, col % 2
    y, zl = row // 2, row % 2

    def at_xz(dx, dz):
        return (((x + dx + 4) % 4) * 4 + ((zh + dz) % 2) * 2 + core, row)

    def at_yz(dy, dz):
        return (col, ((y + dy + 4) % 4) * 2 + (zl + dz) % 2)

    mate = (col + 1 - 2 * core, row)
    up, down, across = at_yz(1, 0), at_yz(-1, 0), at_yz(0, 1)
    right, left, far, over = at_xz(1, 0), at_xz(3, 0), at_xz(2, 0), at_xz(0, 1)

    own = 2 * y + zl
    loads = [
        pltpu.make_async_copy(gv_hbm, g.at[own], in_sem.at[0]),
        pltpu.make_async_copy(ge_hbm, ge, in_sem.at[1]),
        pltpu.make_async_copy(av_hbm, a_own, in_sem.at[2]),
        pltpu.make_async_copy(ae_hbm, ae, in_sem.at[3]),
        pltpu.make_async_copy(wv_hbm, w, in_sem.at[4]),
        pltpu.make_async_copy(we_hbm, we, in_sem.at[5]),
    ]
    for load in loads[:2]:
        load.start()

    barrier = pltpu.get_barrier_semaphore()
    peers = (up, down, across, right, left, far, over, mate)
    for peer in peers:
        pl.semaphore_signal(barrier, inc=1, device_id=peer, device_id_type=MESH)

    spread[...] = spreader(spread.shape[0])

    def block(dy, dz):
        return 2 * ((y + dy + 4) % 4) + (zl + dz) % 2

    def rows_of(q):
        return pl.ds(OFFS[q], SIZES[q])

    def g_copy(link, unit, arriving=False):
        dy, dz, q = LINKS[link][unit]
        if arriving:
            dy, dz = dy + (-1, 1, 0)[link], dz + (0, 0, 1)[link]
        piece = g.at[block(dy, dz), :, rows_of(q)]
        return pltpu.make_async_remote_copy(
            src_ref=piece, dst_ref=piece, send_sem=g_send.at[link, unit], recv_sem=g_recv.at[link, unit],
            device_id=(up, down, across)[link], device_id_type=MESH,
        )

    def g_issue(y_unit=None, z_unit=None):
        for link, unit in ((0, y_unit), (1, y_unit), (2, z_unit)):
            if unit is not None:
                g_copy(link, unit).start()

    def g_arrived(y_unit=None, z_unit=None):
        for link, unit in ((0, y_unit), (1, y_unit), (2, z_unit)):
            if unit is not None:
                g_copy(link, unit, True).wait_recv()

    loads[0].wait()
    loads[1].wait()
    for load in loads[2:]:
        load.start()
    side = g.shape[2]
    for first in range(0, 2 * side, 128):
        scale = factors(ge[:, first : first + 128], spread[...])
        for c in range(2):
            low, high = max(first, c * side), min(first + 128, (c + 1) * side)
            if low < high:
                rows = pl.ds(low - c * side, high - low)
                g[own, c, rows] = g[own, c, rows] * scale[low - first : high - first]
        if first == 128:
            pl.semaphore_wait(barrier, len(peers))
            g_issue(0, 0)
    g_issue(1, 1)

    loads[2].wait()
    loads[3].wait()
    groups = ae.shape[0]
    a_own[...] = a_own[...] * factors(ae[...], spread[:groups, : groups * BLOCK])
    half = a_own.shape[1] // 2
    mine = pl.ds(pl.multiple_of(core * half, half), half)
    theirs = pl.ds(pl.multiple_of((1 - core) * half, half), half)
    pair = pltpu.make_async_remote_copy(
        src_ref=a_own.at[:, theirs], dst_ref=a_pair.at[core], send_sem=pair_send, recv_sem=pair_recv,
        device_id=mate, device_id_type=MESH,
    )
    pair.start()
    a_pair[core] = a_own[:, mine]

    loads[4].wait()
    loads[5].wait()

    def scale_weight(i, carry):
        rows = pl.ds(pl.multiple_of(i * 128, 128), 128)
        w[rows] = w[rows] * factors(we[:, rows], spread[...])
        return carry

    lax.fori_loop(0, w.shape[0] // 128, scale_weight, 0)

    pair.wait()
    at[2 * x + zh, mine] = a_pair[...].reshape(2 * a_pair.shape[1], half).T

    def at_copy(dx, dz, k, device):
        piece = at.at[2 * ((x + dx) % 4) + (zh + dz) % 2, mine]
        return pltpu.make_async_remote_copy(
            src_ref=piece, dst_ref=piece, send_sem=at_send.at[k], recv_sem=at_recv.at[k],
            device_id=device, device_id_type=MESH,
        )

    def mix_copy(dx, dz, to_me=False):
        k = 2 * dx + dz
        piece = at.at[2 * ((x + dx) % 4) + (zh + dz) % 2, theirs if to_me else mine]
        return pltpu.make_async_remote_copy(
            src_ref=piece, dst_ref=piece, send_sem=mix_send.at[k], recv_sem=mix_recv.at[k],
            device_id=mate, device_id_type=MESH,
        )

    at_sent = [at_copy(0, 0, 0, over)] + [at_copy(0, 0, d, at_xz(d, 0)) for d in (1, 3, 2)]
    for copy in at_sent:
        copy.start()
    mixed = [mix_copy(0, 0)]
    mixed[0].start()

    def at_over():
        at_copy(0, 1, 0, over).wait_recv()
        for d in (1, 3, 2):
            at_sent.append(at_copy(0, 1, 3 + d, at_xz(d, 0)))
            at_sent[-1].start()
        mixed.append(mix_copy(0, 1))
        mixed[-1].start()

    def at_line(dz):
        for d in (1, 3, 2):
            at_copy(4 - d, dz, 3 * dz + d, right).wait_recv()
            mixed.append(mix_copy(4 - d, dz))
            mixed[-1].start()

    def at_whole():
        for dx in range(4):
            for dz in range(2):
                mix_copy(dx, dz, True).wait_recv()

    def target(piece):
        return (y + piece[0] + 4) % 4, (zl + piece[1]) % 2

    def size_of(k):
        return sum(SIZES[piece[2]] for piece in JOBS[k])

    def pieces_of(k):
        start = 0
        for i, piece in enumerate(JOBS[k]):
            yield i, piece, start
            start += SIZES[piece[2]]

    def ps_copy(k):
        slot, rows = k % 4, pl.ds(0, size_of(k))
        return pltpu.make_async_remote_copy(
            src_ref=ps.at[slot, 1 - core, rows], dst_ref=pr.at[slot, rows],
            send_sem=ps_send.at[slot], recv_sem=ps_recv.at[slot], device_id=mate, device_id_type=MESH,
        )

    def place(piece):
        xt, zt = target(piece)
        apart = (x - xt + 4) % 4
        return xt, zt, apart, apart // 2

    def relayed(q):
        return SIZES[q] > 16

    def split(q, half, start):
        first = (SIZES[q] + 16) // 32 * 16
        return pl.ds(start + half * first, SIZES[q] - first if half else first)

    def x_peer(there):
        return (((there + 4) % 4) * 4 + zh * 2 + core, row)

    def rr_copy(k, i, piece, start, side):
        xt, zt, _, _ = place(piece)
        q = piece[2]
        return pltpu.make_async_remote_copy(
            src_ref=xs.at[k % 4, split(q, side, start)], dst_ref=rr.at[2 * side + zt, split(q, side, OFFS[q])],
            send_sem=xs_send.at[k % 4, i, side], recv_sem=rr_recv.at[side, zt, q],
            device_id=x_peer(xt + 1 + 2 * side), device_id_type=MESH,
        )

    def xs_copy(k, i, piece, start, side):
        xt, zt, _, _ = place(piece)
        q = piece[2]
        return pltpu.make_async_remote_copy(
            src_ref=xs.at[k % 4, split(q, 1 - side, start)], dst_ref=xr.at[zt, side, split(q, 1 - side, OFFS[q])],
            send_sem=xs_send.at[k % 4, i, 0], recv_sem=xr_recv.at[zt, side, q, 1 - side],
            device_id=x_peer(xt), device_id_type=MESH,
        )

    def xo_copy(k, i, piece, start):
        xt, zt, apart, _ = place(piece)
        q = piece[2]
        seat = (apart + 3) % 4
        return pltpu.make_async_remote_copy(
            src_ref=xs.at[k % 4, pl.ds(start, SIZES[q])], dst_ref=xr.at[zt, seat, rows_of(q)],
            send_sem=xs_send.at[k % 4, i, 0], recv_sem=xr_recv.at[zt, seat, q, 0],
            device_id=x_peer(xt), device_id_type=MESH,
        )

    def rs_copy(piece, side):
        xt, zt, _, _ = place(piece)
        q = piece[2]
        rows = split(q, side, OFFS[q])
        return pltpu.make_async_remote_copy(
            src_ref=rr.at[2 * side + zt, rows], dst_ref=xr.at[zt, side, rows],
            send_sem=rs_send.at[side, zt, q], recv_sem=xr_recv.at[zt, side, q, side],
            device_id=x_peer(xt), device_id_type=MESH,
        )

    def z_copy(q):
        return pltpu.make_async_remote_copy(
            src_ref=zs.at[rows_of(q)], dst_ref=zr.at[rows_of(q)], send_sem=z_send.at[q], recv_sem=z_recv.at[q],
            device_id=over, device_id_type=MESH,
        )

    def compute(k):
        if k >= 4:
            ps_copy(k - 4).wait_send()
        total = size_of(k)

        parts = [g[block(dy, dz), :, rows_of(q)] for dy, dz, q in JOBS[k]]
        lhs = jnp.concatenate(parts, axis=1).reshape(2 * total, g.shape[3])
        part = lax.dot_general(lhs, w[...], (((1,), (1,)), ((), ())), preferred_element_type=F32)
        ps[k % 4, :, pl.ds(0, total)] = part.reshape(2, total, w.shape[0])
        ps_copy(k).start()

    def xs_sent(k):
        for i, piece, start in pieces_of(k):
            apart = place(piece)[2]
            if not relayed(piece[2]):
                @pl.when(apart != 0)
                def _():
                    xo_copy(k, i, piece, start).wait_send()
                continue

            @pl.when(apart == 2)
            def _():
                for side in range(2):
                    rr_copy(k, i, piece, start, side).wait_send()

            for side in range(2):
                @pl.when(apart == 1 + 2 * side)
                def _():
                    xs_copy(k, i, piece, start, side).wait_send()

    def consume(k):
        ps_copy(k).wait_recv()
        if k >= 4:
            xs_sent(k - 4)
        slot = k % 4

        def chip_sum(rows):
            return ps[slot, core, rows] + pr[slot, rows]

        for i, piece, start in pieces_of(k):
            _, zt, apart, _ = place(piece)
            q = piece[2]
            rows = pl.ds(start, SIZES[q])

            @pl.when(apart == 0)
            def _():
                cs[zt, rows_of(q)] = chip_sum(rows)

            if not relayed(q):
                @pl.when(apart != 0)
                def _():
                    xs[slot, rows] = chip_sum(rows).astype(BF16)
                    xo_copy(k, i, piece, start).start()
                continue

            @pl.when(apart == 2)
            def _():
                xs[slot, rows] = chip_sum(rows).astype(BF16)
                for side in range(2):
                    rr_copy(k, i, piece, start, side).start()

            for side in range(2):
                @pl.when(apart == 1 + 2 * side)
                def _():
                    now = split(q, 1 - side, start)
                    xs[slot, now] = chip_sum(now).astype(BF16)
                    xs_copy(k, i, piece, start, side).start()
                    hs[side, zt, split(q, side, OFFS[q])] = chip_sum(split(q, side, start))

    def relay(k):
        for piece in JOBS[k]:
            _, zt, apart, _ = place(piece)
            q = piece[2]
            if not relayed(q):
                continue
            for side in range(2):
                @pl.when(apart == 1 + 2 * side)
                def _():
                    part = split(q, side, OFFS[q])
                    pltpu.make_async_remote_copy(
                        src_ref=rr.at[2 * side + zt, part], dst_ref=rr.at[2 * side + zt, part], send_sem=xs_send.at[0, 0, 0],
                        recv_sem=rr_recv.at[side, zt, q], device_id=right, device_id_type=MESH,
                    ).wait_recv()
                    rr[2 * side + zt, part] = (hs[side, zt, part] + rr[2 * side + zt, part].astype(F32)).astype(BF16)
                    rs_copy(piece, side).start()

    def collect(k):
        for piece in JOBS[k]:
            collect_piece(piece)

    def collect_piece(piece):
        q = piece[2]
        _, zt, apart, _ = place(piece)
        rows = rows_of(q)

        @pl.when(apart == 0)
        def _():
            if relayed(q):
                parts = [(side, half, split(q, half, OFFS[q])) for side in range(2) for half in range(2)]
            else:
                parts = [(seat, 0, rows) for seat in range(3)]
            for seat, half, part in parts:
                pltpu.make_async_remote_copy(
                    src_ref=xr.at[zt, seat, part], dst_ref=xr.at[zt, seat, part], send_sem=xs_send.at[0, 0, 0],
                    recv_sem=xr_recv.at[zt, seat, q, half], device_id=right, device_id_type=MESH,
                ).wait_recv()
            total = cs[zt, rows] + (xr[zt, 0, rows].astype(F32) + xr[zt, 1, rows].astype(F32))
            if not relayed(q):
                total = total + xr[zt, 2, rows].astype(F32)

            @pl.when(zt == zh)
            def _():
                cs[zt, rows] = total

            @pl.when(zt != zh)
            def _():
                zs[rows] = total.astype(BF16)
                z_copy(q).start()

    blocks = {}
    for job in JOBS:
        for piece in job:
            blocks.setdefault(piece[:2], []).append(piece)

    def finish():
        for pieces in blocks.values():
            xt, zt = target(pieces[0])

            @pl.when((xt == x) & (zt == zh))
            def _():
                for piece in pieces:
                    z_copy(piece[2]).wait_recv()
                out[0] = (cs[zh] + zr[...].astype(F32)).astype(BF16)

    def blocks_sent():
        for pieces in blocks.values():
            xt, zt, apart, _ = place(pieces[0])

            @pl.when((apart == 0) & (zt != zh))
            def _():
                for piece in pieces:
                    z_copy(piece[2]).wait_send()

            for side in range(2):
                @pl.when(apart == 1 + 2 * side)
                def _():
                    for piece in pieces:
                        if relayed(piece[2]):
                            rs_copy(piece, side).wait_send()

    def g_sent(low, high):
        for link, units in enumerate(LINKS):
            for unit in range(low, min(high, len(units))):
                g_copy(link, unit).wait_send()

    def tiles(pairs, first, last, low, high):
        blocks = [block(dy, dz) for dy, dz in pairs]
        depth = len(blocks) * g.shape[1] * g.shape[2]

        def part(cols, size):
            lhs = jnp.concatenate([at[b] for b in blocks], axis=1)
            rhs = jnp.concatenate([g[b, :, :, cols] for b in blocks], axis=0).reshape(depth, size)
            value = jnp.dot(lhs, rhs, preferred_element_type=F32)
            if not first:
                value = acc[:, cols] + value
            if last:
                wout[:, cols] = value.astype(BF16)
            else:
                acc[:, cols] = value

        for n in range(low, high):
            part(pl.ds(512 * n, 640 if n == 3 else 512), 640 if n == 3 else 512)

    compute(0)
    g_arrived(0)
    g_issue(2)
    compute(1)
    consume(0)
    consume(1)
    g_arrived(1, 0)
    g_issue(3, 2)
    compute(2)
    consume(2)
    relay(0)
    at_over()
    g_arrived(2, 1)
    g_issue(4, 3)
    compute(3)
    compute(4)
    consume(3)
    relay(1)
    relay(2)
    consume(4)
    at_line(0)
    collect(0)
    g_arrived(3, 2)
    g_issue(5, 4)
    g_issue(None, 5)
    compute(5)
    relay(3)
    relay(4)
    collect(1)
    collect(2)
    consume(5)
    g_arrived(4, 3)
    g_issue(6, 6)
    compute(6)
    relay(5)
    collect(3)
    consume(6)
    collect(4)
    g_arrived(5, 4)
    g_arrived(None, 5)
    g_issue(7, 7)
    compute(7)
    at_line(1)
    relay(6)
    compute(8)
    consume(7)
    collect(5)
    consume(8)
    at_whole()
    near = [(0, 0), (0, 1), (-1, 0), (1, 0)]
    tiles(near, True, False, 0, 2)
    g_arrived(6)
    g_issue(8)
    compute(9)
    relay(7)
    relay(8)
    collect(6)
    consume(9)
    tiles(near, True, False, 2, 3)
    g_arrived(7, 6)
    g_issue(9, 8)
    g_issue(None, 9)
    compute(10)
    relay(9)
    collect(7)
    collect(8)
    consume(10)
    tiles(near, True, False, 3, 4)
    g_sent(0, 7)
    for copy in at_sent + mixed:
        copy.wait_send()
    g_arrived(8, 7)
    g_issue(10)
    compute(11)
    relay(10)
    collect(9)
    consume(11)
    tiles([(2, 0), (2, 1)], False, False, 0, 1)
    g_arrived(9, 8)
    compute(12)
    relay(11)
    collect(10)
    consume(12)
    tiles([(2, 0), (2, 1)], False, False, 1, 2)
    g_arrived(10, 9)
    compute(13)
    tiles([(2, 0), (2, 1)], False, False, 2, 3)
    consume(13)
    collect(11)
    tiles([(2, 0), (2, 1)], False, False, 3, 4)
    rest = [(-1, 1), (1, 1)]
    tiles(rest, False, True, 0, 1)
    collect(12)
    tiles(rest, False, True, 1, 2)
    collect(13)
    tiles(rest, False, True, 2, 3)
    tiles(rest, False, True, 3, 4)
    finish()

    g_sent(7, 11)
    for k in range(len(JOBS) - 4, len(JOBS)):
        ps_copy(k).wait_send()
        xs_sent(k)
    blocks_sent()


def shards(act_values, act_exps, grad_values, grad_exps, weight_values, weight_exps):
    tokens, model = act_values.shape
    rows, width = grad_values.shape
    groups = width // BLOCK
    dma = pltpu.SemaphoreType.DMA
    scratch = [
        pltpu.VMEM((8, 2, rows // 2, width), BF16),
        pltpu.VMEM((8, model, rows), BF16),
        pltpu.VMEM((model, width), BF16),
        pltpu.VMEM((model, width), F32),
        pltpu.VMEM((4, 2, 128, model), F32),
        pltpu.VMEM((4, 128, model), F32),
        pltpu.VMEM((4, 128, model), BF16),
        pltpu.VMEM((2, 3, rows // 2, model), BF16),
        pltpu.VMEM((4, rows // 2, model), BF16),
        pltpu.VMEM((2, 2, rows // 2, model), F32),
        pltpu.VMEM((2, rows // 2, model), F32),
        pltpu.VMEM((rows // 2, model), BF16),
        pltpu.VMEM((rows // 2, model), BF16),
        pltpu.VMEM((groups, rows), jnp.int32),
        pltpu.VMEM((groups, model), jnp.int32),
        pltpu.VMEM((model // BLOCK, tokens), jnp.int32),
        pltpu.VMEM((tokens, model), BF16),
        pltpu.VMEM((2, tokens, model // 2), BF16),
        pltpu.VMEM((groups, width), BF16),
        dma((6,)),
        dma((3, 11)), dma((3, 11)),
        dma, dma,
        dma((7,)), dma((7,)),
        dma((8,)), dma((8,)),
        dma((4,)), dma((4,)),
        dma((4, 3, 2)), dma((2, 3, 12, 2)),
        dma((2, 2, 12)), dma((2, 2, 12)),
        dma((12,)), dma((12,)),
    ]
    anywhere = pl.BlockSpec(memory_space=pl.ANY)
    input_grad, weight_grad = pl.pallas_call(
        kernel,
        out_shape=(pltpu.VMEM((1, tokens, model), BF16), pltpu.VMEM((model, width), BF16)),
        in_specs=[anywhere] * 6,
        out_specs=(pl.BlockSpec(memory_space=pltpu.VMEM),) * 2,
        scratch_shapes=scratch,
        compiler_params=pltpu.CompilerParams(
            collective_id=0, has_side_effects=True, vmem_limit_bytes=58 * 2**20
        ),
        cost_estimate=pl.CostEstimate(
            flops=4 * 8 * rows * model * width, bytes_accessed=16 * 2**20, transcendentals=0
        ),
        name="fused",
    )(
        act_values, act_exps.T,
        grad_values.reshape(2, rows // 2, width), grad_exps.T,
        weight_values, weight_exps.T,
    )
    return input_grad.reshape(tokens, model), weight_grad


def solution(mesh):
    in_specs = (P("col", "row"),) * 2 + (P("row", "col"),) * 4
    out_specs = (P("col", "row"), P("row", "col"))
    return jax.shard_map(shards, mesh=mesh, in_specs=in_specs, out_specs=out_specs, check_vma=False)
```
